256 devices in a mesh: dp: 32 (over z_lo, x, y), tensor: 8 (over z_hi, core).
Axes of the slice: x: 4, y: 4, z: 8 (z_hi: 4, z_lo: 2; z = z_hi * 2 + z_lo), core: 2. Of those that a mesh axis runs over, the one named last changes fastest.
Arguments:
- grad_out: bfloat16 [32768, 6144], P(('dp', 'tensor')), may hold values from -24 to 24
- out_weight: bfloat16 [3072, 6144], P('tensor', 'dp'), may hold values from -0.109375 to 0.109375
- queries: bfloat16 [32768, 3072], P('dp', 'tensor'), may hold values from -21 to 21
- keys_in: bfloat16 [32768, 3072], P('dp', 'tensor'), may hold values from -21 to 21
- values: bfloat16 [32768, 3072], P('dp', 'tensor'), may hold values from -6 to 6
- image_ids: int32 [32768], P('dp'), may hold values from -1 to 2047, as said below
Outputs:
- query_grad: bfloat16 [32768, 3072], P('dp', 'tensor')
- key_grad: bfloat16 [32768, 3072], P('dp', 'tensor')
- value_grad: bfloat16 [32768, 3072], P('dp', 'tensor')
- weight_grad: float32 [3072, 6144], P('tensor', 'dp')
The draws below stay inside these ranges and needn't reach their ends.
Inputs may be any that keep to these rules, and one draw needn't show every extreme that they name: `image_ids`: images are runs of whole 16-token blocks that never cross a 512-token boundary; an image's number is the index of its first 16-token block in the array, so numbers never fall along the array; any token may be dropped.
All inputs are finite; a program needn't handle non-finite values.
Results may differ from the reference program's by a relative error of at most 0.015.
Values may be sent and summed in bfloat16 or wider, within the bound.
A program may use at most 128 MiB of HBM per device.

```python
import jax
import jax.numpy as jnp
from jax import lax

D = 6144
HDIM = 128
BUCKET = 512
IMG_UNIT = 16
TOKENS = 32768
HD = 3072


def image_numbers(key):
    local_key = jax.random.fold_in(key, 11)
    first_key, drop_key = jax.random.split(local_key)
    blocks = TOKENS // IMG_UNIT
    per_bucket = BUCKET // IMG_UNIT
    block_index = jnp.arange(blocks)
    starts = jax.random.randint(first_key, (blocks,), 0, 4) == 0
    forced = (block_index % per_bucket == 0) | (block_index == blocks - 1)
    starts = starts | forced
    first_block = lax.cummax(jnp.where(starts, block_index, 0).astype(jnp.int32), axis=0)
    image_index = jnp.repeat(first_block, IMG_UNIT)
    row_index = jnp.arange(TOKENS)
    dropped = jax.random.randint(drop_key, (TOKENS,), 0, 4) == 0
    dropped = (dropped | (row_index == 1)) & (row_index != TOKENS - 1)
    return jnp.where(dropped, -1, image_index).astype(jnp.int32)


def draw_image_ids(key, part):
    return image_numbers(key)


def draw_queries(key, part):
    key = jax.random.fold_in(key, 5)
    draw_base = jnp.clip(jax.random.normal(key, (TOKENS, HD), jnp.float32), -4.0, 4.0)
    return draw_base.astype(jnp.bfloat16)


def draw_keys_in(key, part):
    key = jax.random.fold_in(key, 7)
    draw_base = jnp.clip(jax.random.normal(key, (TOKENS, HD), jnp.float32), -4.0, 4.0)
    return draw_base.astype(jnp.bfloat16)


def with_spikes(values, rng, source, target, parts, factor):
    owner, partner = [(jnp.arange(values.shape[axis_at]) // (values.shape[axis_at] // parts)).reshape([-1 if axis == axis_at else 1 for axis in range(values.ndim)]) for axis_at in (source, target)]
    chosen = jax.random.permutation(rng, parts)[partner]
    strong = (owner == chosen) | (owner == (partner + parts // 2) % parts)
    return jnp.where(strong, factor * values, values)


def steps_of(own_key, shape, cuts, least, high):
    def one(dim, shards_of):
        heights = jax.random.uniform(jax.random.fold_in(jax.random.fold_in(own_key, 6), dim), (shards_of,), jnp.float32, least / len(cuts), high / len(cuts))
        return jnp.repeat(jnp.exp(heights), shape[dim] // shards_of).reshape((-1,) + (1,) * (len(shape) - dim - 1))

    loudness = one(*cuts[0])
    for cut in cuts[1:]:
        loudness = loudness * one(*cut)
    return loudness


def bell_draw(rng, shape, scale, most, cuts=(), kind=jnp.bfloat16):
    entries = scale * jax.random.normal(rng, shape, jnp.float32)
    if cuts:
        entries = entries * steps_of(rng, shape, cuts, -0.22, 0.18)
    return jnp.clip(entries, -most, most).astype(kind)


def gaussian_with(rng, extent, spread, limit, shards, heavy, dtype=jnp.bfloat16):
    entries = spread * jax.random.normal(rng, extent, jnp.float32)
    if shards:
        entries = entries * steps_of(rng, extent, shards, -0.22, 0.18)
    return jnp.clip(with_spikes(entries, jax.random.fold_in(rng, 3), *heavy), -limit, limit).astype(dtype)


def setup_inputs(seed: int = 0) -> dict:
    arg_keys = jax.random.split(jax.random.key(seed), 7)
    grad_out = gaussian_with(arg_keys[0], (TOKENS, D), 1.0, 24.0, ((0, 256),), (0, 1, 256, 6.0))
    out_weight = bell_draw(arg_keys[1], (HD, D), HD ** -0.5, 0.109375, ((0, 8), (1, 32)))
    queries = draw_queries(jax.random.fold_in(arg_keys[6], 71), 0)
    keys_in = draw_keys_in(jax.random.fold_in(arg_keys[6], 71), 0)
    values = bell_draw(arg_keys[4], (TOKENS, HD), 1.0, 6.0, ((0, 32), (1, 8)))
    image_ids = draw_image_ids(jax.random.fold_in(arg_keys[6], 71), 0)
    return {"grad_out": grad_out, "out_weight": out_weight, "queries": queries, "keys_in": keys_in, "values": values, "image_ids": image_ids}


masked_value = -1e30


def bucket_pass(bundle):
    query_rows, key_rows, value_rows, grad_rows, segments = bundle
    head_count = query_rows.shape[1] // HDIM

    def split_heads(matrix):
        return matrix.reshape(BUCKET, head_count, HDIM).transpose(1, 0, 2).astype(jnp.float32)

    def join_heads(matrix):
        return matrix.transpose(1, 0, 2).reshape(BUCKET, head_count * HDIM)

    query_block = split_heads(query_rows)
    key_block = split_heads(key_rows)
    value_block = split_heads(value_rows)
    grad_block = split_heads(grad_rows)
    score_scale = HDIM ** -0.5
    position = jnp.arange(BUCKET)
    same_image = (segments[:, None] == segments[None, :]) & (segments[:, None] >= 0)
    allowed = same_image | (position[:, None] == position[None, :])
    raw_scores = jnp.einsum("hqd,hkd->hqk", query_block, key_block) * score_scale
    scores = jnp.where(allowed[None], raw_scores, masked_value)
    row_top = jnp.max(scores, axis=-1)
    log_total = row_top + jnp.log(jnp.sum(jnp.exp(scores - row_top[..., None]), axis=-1))
    probabilities = jnp.exp(scores - log_total[..., None])
    prob_bf = lax.optimization_barrier(probabilities.astype(jnp.bfloat16)).astype(jnp.float32)
    attn_out = jnp.einsum("hqk,hkd->hqd", prob_bf, value_block).astype(jnp.bfloat16)
    attn_wide = lax.optimization_barrier(attn_out).astype(jnp.float32)
    row_delta = jnp.sum(grad_block * attn_wide, axis=-1)
    prob_grad = jnp.einsum("hqd,hkd->hqk", grad_block, value_block)
    score_grad = (probabilities * (prob_grad - row_delta[..., None])).astype(jnp.bfloat16)
    score_grad = lax.optimization_barrier(score_grad).astype(jnp.float32)
    query_grad = (jnp.einsum("hqk,hkd->hqd", score_grad, key_block) * score_scale).astype(jnp.bfloat16)
    key_grad = (jnp.einsum("hqk,hqd->hkd", score_grad, query_block) * score_scale).astype(jnp.bfloat16)
    value_grad = jnp.einsum("hqk,hqd->hkd", prob_bf, grad_block).astype(jnp.bfloat16)
    return join_heads(attn_out), join_heads(query_grad), join_heads(key_grad), join_heads(value_grad)


def reference(grad_out, out_weight, queries, keys_in, values, image_ids):
    head_grad = jnp.dot(grad_out, out_weight.T, preferred_element_type=jnp.float32).astype(jnp.bfloat16)
    bucket_total = TOKENS // BUCKET

    def stacked(matrix):
        return matrix.reshape(bucket_total, BUCKET, matrix.shape[1])

    outputs = lax.map(bucket_pass, (stacked(queries), stacked(keys_in), stacked(values), stacked(head_grad), image_ids.reshape(bucket_total, BUCKET)))
    attn_out, query_grad, key_grad, value_grad = [piece_out.reshape(TOKENS, HD) for piece_out in outputs]
    weight_grad = jnp.dot(attn_out.T, grad_out, preferred_element_type=jnp.float32)
    return query_grad, key_grad, value_grad, weight_grad
```

```python
import jax
import jax.numpy as jnp
from jax import lax
from jax.sharding import PartitionSpec as P
import jax.experimental.pallas as pl
import jax.experimental.pallas.tpu as pltpu

HDIM = 128
BUCKET = 512
ROWS = 1024
SUB = 128
WIDTH = 6144
COLS = 384
SHARD = 192
STEPS = 16
AHEAD = 3
MESH = pl.DeviceIdType.MESH
BF = jnp.bfloat16
F32 = jnp.float32
masked_value = -1e30
score_scale = HDIM ** (-0.5)


def dot(a, b, da, db):
    return lax.dot_general(a, b, (((da,), (db,)), ((), ())), preferred_element_type=F32)


def kernel(
    grad_hbm, weight_ref, q_ref, k_ref, v_ref, ids_ref,
    dq_ref, dk_ref, dv_ref, wg_ref,
    grad, weight, attn_t, prob_t, head_grad, stage, parts, pair_out, pair_in,
    local_sem, own_send, own_recv, fwd_send, fwd_recv, sib_send, sib_recv,
    w_send, w_recv, part_send, part_recv, pair_send, pair_recv,
):
    dp = lax.axis_index("dp")
    tensor = lax.axis_index("tensor")
    zl, x, y = dp // 16, (dp // 4) % 4, dp % 4
    zh, core = tensor // 2, tensor % 2
    here = x * 4 + y
    up, down, far = (zh + 1) % 4, (zh + 3) % 4, (zh + 2) % 4
    up_id, down_id = (dp, up * 2 + core), (dp, down * 2 + core)
    sib_id = (dp, zh * 2 + 1 - core)
    pair_id = ((1 - zl) * 16 + here, tensor)

    def plane_id(px, py):
        return (zl * 16 + px * 4 + py, tensor)

    def remote(src, dst, send, recv, device):
        return pltpu.make_async_remote_copy(
            src_ref=src, dst_ref=dst, send_sem=send, recv_sem=recv,
            device_id=device, device_id_type=MESH,
        )

    def place(s):
        group = s // 8
        zc = jnp.where(group == 0, 1 - zl, zl)
        xc = (x + 3 - (s % 8) // 2) % 4
        half = s % 2
        return group, zc, xc, half

    def offset(s):
        _, zc, xc, half = place(s)
        return pl.multiple_of((zc * 4 + xc) * 768 + half * COLS, COLS)

    def block(z, s, first=0, rows=SUB):
        start = pl.multiple_of((z * 2 + core) * SUB + first, rows)
        return grad.at[pl.ds(start, rows), pl.ds(offset(s), COLS)]

    def own_copy(s, way):
        part = block(zh, s)
        return remote(part, part, own_send.at[way, s], own_recv.at[way, s], (up_id, down_id)[way])

    def own_arrival(s, way):
        part = block((down, up)[way], s)
        return remote(part, part, own_send.at[way, s], own_recv.at[way, s], (up_id, down_id)[way])

    def fwd_copy(s, way):
        part = block((down, up)[way], s, way * 64, 64)
        return remote(part, part, fwd_send.at[way, s], fwd_recv.at[way, s], (up_id, down_id)[way])

    def fwd_arrival(s, way):
        part = block(far, s, way * 64, 64)
        return remote(part, part, fwd_send.at[way, s], fwd_recv.at[way, s], (up_id, down_id)[way])

    def sib_copy(s, n):
        part = block((zh, down, up, far)[n], s)
        return remote(part, part, sib_send.at[n, s], sib_recv.at[n, s], sib_id)

    def sib_arrival(s, n):
        z = (zh, down, up, far)[n]
        start = pl.multiple_of((z * 2 + 1 - core) * SUB, SUB)
        part = grad.at[pl.ds(start, SUB), pl.ds(offset(s), COLS)]
        return remote(part, part, sib_send.at[n, s], sib_recv.at[n, s], sib_id)

    def w_slot(slot):
        return weight.at[pl.ds(pl.multiple_of(slot * SHARD, SHARD), SHARD), :]

    def w_copy(group, m):
        slot = jnp.where(group == 0, 1 - zl, zl) * 16 + here
        px, py = (x + 1 + m // 4) % 4, (y + m) % 4
        return remote(
            w_slot(slot), w_slot(slot), w_send.at[group, m], w_recv.at[slot], plane_id(px, py)
        )

    def pair_w():
        slot = dp
        return remote(w_slot(slot), w_slot(slot), w_send.at[1, 12], w_recv.at[slot], pair_id)

    def w_arrival(slot):
        return remote(w_slot(slot), w_slot(slot), w_send.at[0, 0], w_recv.at[slot], pair_id)

    def part_copy(s, n):
        group, zc, xc, half = place(s)
        return remote(
            stage.at[s, pl.ds(n * SHARD, SHARD), :], parts.at[group, here],
            part_send.at[s, n], part_recv.at[group, here], plane_id(xc, half * 2 + n),
        )

    def part_arrival(group, source):
        return remote(
            parts.at[group, source], parts.at[group, source],
            part_send.at[0, 0], part_recv.at[group, source], pair_id,
        )

    def pair_copy():
        return remote(pair_out, pair_in, pair_send, pair_recv, pair_id)

    load = pltpu.make_async_copy(
        grad_hbm, grad.at[pl.ds(pl.multiple_of(tensor * SUB, SUB), SUB), :], local_sem
    )
    load.start()

    barrier = pltpu.get_barrier_semaphore()
    for device in (up_id, down_id, sib_id, pair_id):
        pl.semaphore_signal(barrier, inc=1, device_id=device, device_id_type=MESH)
    for m in range(16):
        if m != 12:
            pl.semaphore_signal(
                barrier, inc=1, device_id=plane_id((x + 1 + m // 4) % 4, (y + m) % 4),
                device_id_type=MESH,
            )
    weight[pl.ds(pl.multiple_of(dp * SHARD, SHARD), SHARD), :] = weight_ref[...]
    load.wait()
    pl.semaphore_wait(barrier, 19)

    @pl.loop(0, AHEAD)
    def _(s):
        own_copy(s, 0).start()
        own_copy(s, 1).start()

    pair_w().start()

    @pl.loop(0, 16)
    def _(m):
        @pl.when(m != 12)
        def _():
            w_copy(1, m).start()

    @pl.loop(0, STEPS)
    def _(s):
        sib_copy(s, 0).start()

    w_arrival((1 - zl) * 16 + here).wait_recv()

    @pl.loop(0, 16)
    def _(m):
        @pl.when(m != 12)
        def _():
            w_copy(0, m).start()

    def head_slices(i):
        bucket, head = i // 3, i % 3
        rows = pl.ds(pl.multiple_of(bucket * BUCKET, BUCKET), BUCKET)
        cols = pl.ds(pl.multiple_of(head * HDIM, HDIM), HDIM)
        return bucket, rows, cols

    @pl.loop(0, 6)
    def _(i):
        bucket, rows, cols = head_slices(i)
        ids = ids_ref[bucket]
        position = lax.broadcasted_iota(jnp.int32, (1, BUCKET), 1)
        label = jnp.where(ids < 0, -1 - position, ids).astype(F32)
        column = jnp.broadcast_to(label, (HDIM, BUCKET)).T
        column = jnp.concatenate([column] * (BUCKET // HDIM), axis=1)
        scores = dot(k_ref[rows, cols], q_ref[rows, cols], 1, 1) * score_scale
        scores = jnp.where(column == label, scores, masked_value)
        weights = jnp.exp(scores - jnp.max(scores, axis=0, keepdims=True))
        prob = weights / jnp.sum(weights, axis=0, keepdims=True)
        prob_t[i] = prob
        attn_t[cols, rows] = dot(v_ref[rows, cols], prob.astype(BF), 0, 0).astype(BF)

    head_grad[...] = jnp.zeros_like(head_grad)

    def matmuls(s):
        at = offset(s)
        group, zc, xc, half = place(s)
        w_part = weight[pl.ds(at, COLS), :]
        for t in range(4):
            rows = pl.ds(t * 256, 256)
            head_grad[rows, :] += dot(grad[rows, pl.ds(at, COLS)], w_part, 1, 0)
        for h in range(3):
            part = dot(attn_t[h * HDIM:(h + 1) * HDIM, :], grad[:, pl.ds(at, COLS)], 1, 0)
            stage[s, :, h * HDIM:(h + 1) * HDIM] = part.T.astype(BF)
        for n in range(2):
            mine = (xc == x) & (half * 2 + n == y)

            @pl.when(mine)
            def _():
                parts[group, here] = stage[s, n * SHARD:(n + 1) * SHARD, :]

            @pl.when(jnp.logical_not(mine))
            def _():
                part_copy(s, n).start()

    def collect(group):
        @pl.loop(0, 16)
        def _(source):
            @pl.when(source != here)
            def _():
                part_arrival(group, source).wait_recv()

    def part_sum(group, rows):
        def add(source, total):
            return total + parts[group, source, rows, :].astype(F32)

        return lax.fori_loop(0, 16, add, jnp.zeros((48, COLS), F32))

    @pl.loop(0, STEPS + 1)
    def _(s):
        @pl.when(s < STEPS)
        def _():
            own_arrival(s, 0).wait_recv()
            own_arrival(s, 1).wait_recv()
            fwd_copy(s, 0).start()
            fwd_copy(s, 1).start()
            sib_copy(s, 1).start()
            sib_copy(s, 2).start()

        @pl.when(s + AHEAD < STEPS)
        def _():
            own_copy(s + AHEAD, 0).start()
            own_copy(s + AHEAD, 1).start()

        @pl.when(s >= 1)
        def _():
            t = s - 1
            fwd_arrival(t, 0).wait_recv()
            fwd_arrival(t, 1).wait_recv()
            sib_copy(t, 3).start()
            group, zc, xc, half = place(t)
            for n in range(2):
                yc = half * 2 + n

                @pl.when((xc != x) | (yc != y))
                def _():
                    w_arrival(zc * 16 + xc * 4 + yc).wait_recv()

            for n in range(4):
                sib_arrival(t, n).wait_recv()
            matmuls(t)

        @pl.when(s == 12)
        def _():
            collect(0)

            @pl.loop(0, 4)
            def _(r):
                rows = pl.ds(pl.multiple_of(r * 48, 48), 48)
                pair_out[rows, :] = part_sum(0, rows).astype(BF)

            pair_copy().start()

    @pl.loop(0, 6)
    def _(i):
        bucket, rows, cols = head_slices(i)
        grad_h = head_grad[rows, cols].astype(BF)
        prob = prob_t[i]
        prob_grad = dot(v_ref[rows, cols], grad_h, 1, 1)
        delta = jnp.sum(
            grad_h.astype(F32).T * attn_t[cols, rows].astype(F32), axis=0, keepdims=True
        )
        score_grad = (prob * (prob_grad - delta)).astype(BF)
        dv_ref[rows, cols] = dot(prob.astype(BF), grad_h, 1, 0).astype(BF)
        dk_ref[rows, cols] = (dot(score_grad, q_ref[rows, cols], 1, 0) * score_scale).astype(BF)
        dq = dot(k_ref[rows, cols], score_grad, 0, 0) * score_scale
        dq_ref[rows, cols] = dq.T.astype(BF)

    collect(1)
    pair_copy().wait_recv()

    @pl.loop(0, 4)
    def _(r):
        rows = pl.ds(pl.multiple_of(r * 48, 48), 48)
        wg_ref[rows, :] = part_sum(1, rows) + pair_in[rows, :].astype(F32)

    pair_copy().wait_send()
    pair_w().wait_send()

    @pl.loop(0, 16)
    def _(m):
        @pl.when(m != 12)
        def _():
            w_copy(0, m).wait_send()
            w_copy(1, m).wait_send()

    @pl.loop(0, STEPS)
    def _(s):
        for way in range(2):
            own_copy(s, way).wait_send()
            fwd_copy(s, way).wait_send()
        for n in range(4):
            sib_copy(s, n).wait_send()
        group, zc, xc, half = place(s)
        for n in range(2):
            @pl.when((xc != x) | (half * 2 + n != y))
            def _():
                part_copy(s, n).wait_send()


def on_device(grad_out, out_weight, queries, keys_in, values, image_ids):
    vmem = pl.BlockSpec(memory_space=pltpu.VMEM)
    dma = pltpu.SemaphoreType.DMA
    outs = pl.pallas_call(
        kernel,
        out_shape=(
            jax.ShapeDtypeStruct((ROWS, COLS), BF),
            jax.ShapeDtypeStruct((ROWS, COLS), BF),
            jax.ShapeDtypeStruct((ROWS, COLS), BF),
            jax.ShapeDtypeStruct((SHARD, COLS), F32),
        ),
        in_specs=[pl.BlockSpec(memory_space=pl.ANY)] + [vmem] * 5,
        out_specs=(vmem,) * 4,
        scratch_shapes=[
            pltpu.VMEM((ROWS, WIDTH), BF),
            pltpu.VMEM((WIDTH, COLS), BF),
            pltpu.VMEM((COLS, ROWS), BF),
            pltpu.VMEM((6, BUCKET, BUCKET), F32),
            pltpu.VMEM((ROWS, COLS), F32),
            pltpu.VMEM((STEPS, COLS, COLS), BF),
            pltpu.VMEM((2, 16, SHARD, COLS), BF),
            pltpu.VMEM((SHARD, COLS), BF),
            pltpu.VMEM((SHARD, COLS), BF),
            dma,
            dma((2, STEPS)), dma((2, STEPS)),
            dma((2, STEPS)), dma((2, STEPS)),
            dma((4, STEPS)), dma((4, STEPS)),
            dma((2, 16)), dma((32,)),
            dma((STEPS, 2)), dma((2, 16)),
            dma, dma,
        ],
        compiler_params=pltpu.CompilerParams(
            collective_id=0, has_side_effects=True, vmem_limit_bytes=60 * 2**20
        ),
        cost_estimate=pl.CostEstimate(
            flops=13 * 10**9, bytes_accessed=30 * 10**6, transcendentals=1572864
        ),
        name="attention_backward",
    )(
        grad_out, out_weight.T, queries, keys_in, values,
        image_ids.reshape(2, 1, BUCKET),
    )
    return (outs[0], outs[1], outs[2], outs[3].T)


def solution(mesh):
    placed = (
        P(("dp", "tensor"), None),
        P("tensor", "dp"),
        P("dp", "tensor"),
        P("dp", "tensor"),
        P("dp", "tensor"),
        P("dp"),
    )
    return jax.shard_map(
        on_device,
        mesh=mesh,
        in_specs=placed,
        out_specs=(P("dp", "tensor"), P("dp", "tensor"), P("dp", "tensor"), P("tensor", "dp")),
        check_vma=False,
    )
```

```python
import jax
import jax.numpy as jnp
from jax import lax
from jax.sharding import PartitionSpec as P
import jax.experimental.pallas as pl
import jax.experimental.pallas.tpu as pltpu

HDIM = 128
BUCKET = 512
ROWS = 1024
SUB = 128
WIDTH = 6144
COLS = 384
SHARD = 192
STEPS = 16
AHEAD = 3
MESH = pl.DeviceIdType.MESH
BF = jnp.bfloat16
F32 = jnp.float32
masked_value = -1e30
score_scale = HDIM ** (-0.5)


def dot(a, b, da, db):
    return lax.dot_general(a, b, (((da,), (db,)), ((), ())), preferred_element_type=F32)


def kernel(
    grad_hbm, q_hbm, k_hbm, v_hbm, weight_ref, ids_ref,
    dq_hbm, dk_hbm, dv_hbm, wg_ref,
    grad, weight, attn_t, prob_t, head_grad, stage, parts, pair_out, pair_in, early_sum,
    q_ref, k_ref, v_ref, dq_ref, dk_ref, dv_ref, local_sem, in_sem, out_sem, hop_send, hop_recv, sib_send, sib_recv,
    w_send, w_recv, part_send, part_recv, pair_send, pair_recv,
):
    dp = lax.axis_index("dp")
    tensor = lax.axis_index("tensor")
    zl, x, y = dp // 16, (dp // 4) % 4, dp % 4
    zh, core = tensor // 2, tensor % 2
    here = x * 4 + y
    u, v = jnp.where(core == 0, x, y), jnp.where(core == 0, y, x)
    up, down, far = (zh + 1) % 4, (zh + 3) % 4, (zh + 2) % 4
    ahead, back = jnp.where(core == 0, up, down), jnp.where(core == 0, down, up)
    next_id = (dp, ahead * 2 + core)
    up_id, down_id = (dp, up * 2 + core), (dp, down * 2 + core)
    sib_id = (dp, zh * 2 + 1 - core)
    pair_id = ((1 - zl) * 16 + here, tensor)

    def plane_id(px, py):
        return (zl * 16 + px * 4 + py, tensor)

    def remote(src, dst, send, recv, device):
        return pltpu.make_async_remote_copy(
            src_ref=src, dst_ref=dst, send_sem=send, recv_sem=recv,
            device_id=device, device_id_type=MESH,
        )

    def place(s):
        group = s // 8
        zc = jnp.where(group == 0, 1 - zl, zl)
        xc = (x + 3 - (s % 8) // 2) % 4
        half = (s + 1 + y // 2) % 2
        return group, zc, xc, half

    def chunk(s):
        _, zc, xc, half = place(s)
        return (zc * 4 + xc) * 2 + half

    def block(z, s, first=0, rows=SUB):
        start = pl.multiple_of((z * 2 + core) * SUB + first, rows)
        return grad.at[chunk(s), pl.ds(start, rows), :]

    def hop_copy(s, n):
        part = block((zh, back, far)[n], s)
        return remote(part, part, hop_send.at[n, s], hop_recv.at[n, s], next_id)

    def hop_arrival(s, n):
        part = block((back, far, ahead)[n], s)
        return remote(part, part, hop_send.at[n, s], hop_recv.at[n, s], next_id)

    def sib_copy(s, n):
        part = block((zh, back, far, ahead)[n], s)
        return remote(part, part, sib_send.at[n, s], sib_recv.at[n, s], sib_id)

    def sib_arrival(s, n):
        z = (zh, back, far, ahead)[n]
        start = pl.multiple_of((z * 2 + 1 - core) * SUB, SUB)
        part = grad.at[chunk(s), pl.ds(start, SUB), :]
        return remote(part, part, sib_send.at[n, s], sib_recv.at[n, s], sib_id)

    def w_slot(slot):
        return weight.at[pl.ds(pl.multiple_of(slot * SHARD, SHARD), SHARD), :]

    def spot(u_at, v_at):
        return jnp.where(core == 0, u_at * 4 + v_at, v_at * 4 + u_at)

    def w_copy(group, m):
        zc = jnp.where(group == 0, 1 - zl, zl)
        first = m // 4 == 0
        slot = w_slot(zc * 16 + spot(u, jnp.where(first, v, (v + m) % 4)))
        to = spot((u + m // 4) % 4, jnp.where(first, (v + m) % 4, v))
        return remote(
            slot, slot, w_send.at[group, m],
            w_recv.at[zc * 16 + spot(u, jnp.where(first, v, (v + m) % 4))], (zl * 16 + to, tensor),
        )

    def w_first(group):
        for m in range(1, 4):
            w_copy(group, m).start()

    def w_second(group):
        zc = jnp.where(group == 0, 1 - zl, zl)
        for m in range(1, 4):
            w_arrival(zc * 16 + spot(u, (v + m) % 4)).wait_recv()

        @pl.loop(4, 16)
        def _(m):
            w_copy(group, m).start()

    def pair_w():
        slot = dp
        return remote(w_slot(slot), w_slot(slot), w_send.at[1, 0], w_recv.at[slot], pair_id)

    def w_arrival(slot):
        return remote(w_slot(slot), w_slot(slot), w_send.at[0, 0], w_recv.at[slot], pair_id)

    def part_copy(s, n):
        group, zc, xc, half = place(s)
        return remote(
            stage.at[s, pl.ds(n * SHARD, SHARD), :], parts.at[group, here],
            part_send.at[s, n], part_recv.at[group, here], plane_id(xc, half * 2 + n),
        )

    def part_arrival(group, source):
        return remote(
            parts.at[group, source], parts.at[group, source],
            part_send.at[0, 0], part_recv.at[group, source], pair_id,
        )

    def pair_copy():
        return remote(pair_out, pair_in, pair_send, pair_recv, pair_id)

    def load(s):
        return pltpu.make_async_copy(
            grad_hbm.at[:, pl.ds(pl.multiple_of(chunk(s) * COLS, COLS), COLS)],
            block(zh, s), local_sem.at[s],
        )

    @pl.loop(0, STEPS)
    def _(s):
        load(s).start()

    heads_in = [
        pltpu.make_async_copy(src, dst, in_sem.at[n])
        for n, (src, dst) in enumerate(((q_hbm, q_ref), (k_hbm, k_ref), (v_hbm, v_ref)))
    ]
    heads_out = [
        pltpu.make_async_copy(src, dst, out_sem.at[n])
        for n, (src, dst) in enumerate(((dq_ref, dq_hbm), (dk_ref, dk_hbm), (dv_ref, dv_hbm)))
    ]
    barrier = pltpu.get_barrier_semaphore()
    for device in (up_id, down_id, sib_id, pair_id):
        pl.semaphore_signal(barrier, inc=1, device_id=device, device_id_type=MESH)
    for m in range(16):
        if m != 12:
            pl.semaphore_signal(
                barrier, inc=1, device_id=plane_id((x + 1 + m // 4) % 4, (y + m) % 4),
                device_id_type=MESH,
            )
    for copy in heads_in:
        copy.start()
    weight[pl.ds(pl.multiple_of(dp * SHARD, SHARD), SHARD), :] = weight_ref[...]
    @pl.loop(0, STEPS)
    def _(s):
        load(s).wait()

    pl.semaphore_wait(barrier, 19)

    @pl.loop(0, AHEAD)
    def _(s):
        hop_copy(s, 0).start()

    pair_w().start()

    w_first(1)

    @pl.loop(0, STEPS)
    def _(s):
        sib_copy(s, 0).start()

    w_arrival((1 - zl) * 16 + here).wait_recv()
    w_first(0)

    def head_slices(i):
        bucket, head = i // 3, i % 3
        rows = pl.ds(pl.multiple_of(bucket * BUCKET, BUCKET), BUCKET)
        cols = pl.ds(pl.multiple_of(head * HDIM, HDIM), HDIM)
        return bucket, rows, cols

    for copy in heads_in:
        copy.wait()

    @pl.loop(0, 6)
    def _(i):
        bucket, rows, cols = head_slices(i)
        ids = ids_ref[bucket]
        position = lax.broadcasted_iota(jnp.int32, (1, BUCKET), 1)
        label = jnp.where(ids < 0, -1 - position, ids).astype(F32)
        column = jnp.broadcast_to(label, (HDIM, BUCKET)).T
        column = jnp.concatenate([column] * (BUCKET // HDIM), axis=1)
        scores = dot(k_ref[rows, cols], q_ref[rows, cols], 1, 1) * score_scale
        scores = jnp.where(column == label, scores, masked_value)
        weights = jnp.exp(scores - jnp.max(scores, axis=0, keepdims=True))
        prob = weights / jnp.sum(weights, axis=0, keepdims=True)
        prob_t[i] = prob
        attn_t[cols, rows] = dot(v_ref[rows, cols], prob.astype(BF), 0, 0).astype(BF)

    head_grad[...] = jnp.zeros_like(head_grad)

    def weight_part(s):
        at = chunk(s)
        group, zc, xc, half = place(s)
        for h in range(3):
            part = dot(attn_t[h * HDIM:(h + 1) * HDIM, :], grad[at], 1, 0)
            stage[s, :, h * HDIM:(h + 1) * HDIM] = part.T.astype(BF)
        for n in range(2):
            mine = (xc == x) & (half * 2 + n == y)

            @pl.when(mine)
            def _():
                parts[group, here] = stage[s, n * SHARD:(n + 1) * SHARD, :]

            @pl.when(jnp.logical_not(mine))
            def _():
                part_copy(s, n).start()

    def head_part(s):
        at = chunk(s)
        group, zc, xc, half = place(s)
        for n in range(2):
            yc = half * 2 + n

            @pl.when(jnp.where(core == 0, xc, yc) != u)
            def _():
                w_arrival(zc * 16 + xc * 4 + yc).wait_recv()

        w_part = weight[pl.ds(pl.multiple_of(at * COLS, COLS), COLS), :]
        for t in range(4):
            rows = pl.ds(t * 256, 256)
            head_grad[rows, :] += dot(grad[at, rows, :], w_part, 1, 0)

    def source_at(i):
        return ((x + 1 + i // 4) % 4) * 4 + i % 4

    def collect(group, first, last):
        @pl.loop(first, last)
        def _(i):
            @pl.when(source_at(i) != here)
            def _():
                part_arrival(group, source_at(i)).wait_recv()

    def part_sum(group, rows, first, last):
        def add(i, total):
            return total + parts[group, source_at(i), rows, :].astype(F32)

        return lax.fori_loop(first, last, add, jnp.zeros((48, COLS), F32))

    def sent(s):
        for n in range(3):
            hop_copy(s, n).wait_send()
        for n in range(4):
            sib_copy(s, n).wait_send()
        group, zc, xc, half = place(s)
        for n in range(2):
            @pl.when((xc != x) | (half * 2 + n != y))
            def _():
                part_copy(s, n).wait_send()

    @pl.loop(0, STEPS + 2)
    def _(s):
        @pl.when(s < STEPS)
        def _():
            hop_arrival(s, 0).wait_recv()
            hop_copy(s, 1).start()
            sib_copy(s, 1).start()

        @pl.when((s >= 1) & (s <= STEPS))
        def _():
            hop_arrival(s - 1, 1).wait_recv()
            hop_copy(s - 1, 2).start()
            sib_copy(s - 1, 2).start()

        @pl.when(s == 1)
        def _():
            w_second(0)

        @pl.when(s == 2)
        def _():
            w_second(1)

        @pl.when(s + AHEAD < STEPS)
        def _():
            hop_copy(s + AHEAD, 0).start()

        @pl.when(s >= 2)
        def _():
            t = s - 2
            hop_arrival(t, 2).wait_recv()
            sib_copy(t, 3).start()
            for n in range(4):
                sib_arrival(t, n).wait_recv()
            weight_part(t)

        @pl.when(s > 9)
        def _():
            @pl.loop(jnp.where(s == STEPS + 1, 15, 2 * s - 20), jnp.where(s == STEPS, 15, 2 * s - 18))
            def _(r):
                head_part(r)

        @pl.when(s == 13)
        def _():
            pair_w().wait_send()

            @pl.loop(1, 16)
            def _(m):
                w_copy(0, m).wait_send()
                w_copy(1, m).wait_send()

        @pl.when(s == 14)
        def _():
            collect(0, 0, 16)

            @pl.loop(0, 4)
            def _(r):
                rows = pl.ds(pl.multiple_of(r * 48, 48), 48)
                pair_out[rows, :] = part_sum(0, rows, 0, 16).astype(BF)

            pair_copy().start()

        @pl.when(s == STEPS)
        def _():
            collect(1, 0, 12)

            @pl.loop(0, 4)
            def _(r):
                rows = pl.ds(pl.multiple_of(r * 48, 48), 48)
                early_sum[rows, :] = part_sum(1, rows, 0, 12)

    @pl.loop(0, 6, unroll=2)
    def _(i):
        bucket, rows, cols = head_slices(i)
        grad_h = head_grad[rows, cols].astype(BF)
        prob = prob_t[i]
        prob_grad = dot(v_ref[rows, cols], grad_h, 1, 1)
        delta = jnp.sum(
            grad_h.astype(F32).T * attn_t[cols, rows].astype(F32), axis=0, keepdims=True
        )
        score_grad = (prob * (prob_grad - delta)).astype(BF)
        dv_ref[rows, cols] = dot(prob.astype(BF), grad_h, 1, 0).astype(BF)
        dk_ref[rows, cols] = (dot(score_grad, q_ref[rows, cols], 1, 0) * score_scale).astype(BF)
        dq = dot(k_ref[rows, cols], score_grad, 0, 0) * score_scale
        dq_ref[rows, cols] = dq.T.astype(BF)

    for copy in heads_out:
        copy.start()
    collect(1, 12, 16)
    pair_copy().wait_recv()

    @pl.loop(0, 4)
    def _(r):
        rows = pl.ds(pl.multiple_of(r * 48, 48), 48)
        late = part_sum(1, rows, 12, 16) + pair_in[rows, :].astype(F32)
        wg_ref[rows, :] = early_sum[rows, :] + late

    for copy in heads_out:
        copy.wait()
    pair_copy().wait_send()

    @pl.loop(0, STEPS)
    def _(s):
        sent(s)


def place_outputs(*refs):
    ins, outs, held, sems = refs[:4], refs[4:8], refs[8:12], refs[12]
    loads = [pltpu.make_async_copy(ins[n], held[n], sems.at[0, n]) for n in range(4)]
    stores = [pltpu.make_async_copy(held[n], outs[n], sems.at[1, n]) for n in range(4)]
    for copy in loads:
        copy.start()
    for n in range(4):
        loads[n].wait()
        stores[n].start()
    for copy in stores:
        copy.wait()


def on_device(grad_out, out_weight, queries, keys_in, values, image_ids):
    vmem = pl.BlockSpec(memory_space=pltpu.VMEM)
    hbm = pl.BlockSpec(memory_space=pl.ANY)
    dma = pltpu.SemaphoreType.DMA
    outs = pl.pallas_call(
        kernel,
        out_shape=(
            jax.ShapeDtypeStruct((ROWS, COLS), BF),
            jax.ShapeDtypeStruct((ROWS, COLS), BF),
            jax.ShapeDtypeStruct((ROWS, COLS), BF),
            jax.ShapeDtypeStruct((SHARD, COLS), F32),
        ),
        in_specs=[hbm] * 4 + [vmem] * 2,
        out_specs=(hbm,) * 3 + (vmem,),
        scratch_shapes=[
            pltpu.VMEM((STEPS, ROWS, COLS), BF),
            pltpu.VMEM((WIDTH, COLS), BF),
            pltpu.VMEM((COLS, ROWS), BF),
            pltpu.VMEM((6, BUCKET, BUCKET), F32),
            pltpu.VMEM((ROWS, COLS), F32),
            pltpu.VMEM((STEPS, COLS, COLS), BF),
            pltpu.VMEM((2, 16, SHARD, COLS), BF),
            pltpu.VMEM((SHARD, COLS), BF),
            pltpu.VMEM((SHARD, COLS), BF),
            pltpu.VMEM((SHARD, COLS), F32),
        ] + [pltpu.VMEM((ROWS, COLS), BF)] * 6 + [
            dma((STEPS,)), dma((3,)), dma((3,)),
            dma((3, STEPS)), dma((3, STEPS)),
            dma((4, STEPS)), dma((4, STEPS)),
            dma((2, 16)), dma((32,)),
            dma((STEPS, 2)), dma((2, 16)),
            dma, dma,
        ],
        compiler_params=pltpu.CompilerParams(
            collective_id=0, has_side_effects=True, vmem_limit_bytes=60 * 2**20
        ),
        cost_estimate=pl.CostEstimate(
            flops=13 * 10**9, bytes_accessed=30 * 10**6, transcendentals=1572864
        ),
        name="attention_backward",
    )(
        grad_out, queries, keys_in, values, out_weight.T,
        image_ids.reshape(2, 1, BUCKET),
    )
    outs = pl.pallas_call(
        place_outputs,
        out_shape=tuple(jax.ShapeDtypeStruct(out.shape, out.dtype) for out in outs),
        in_specs=[hbm] * 4,
        out_specs=(hbm,) * 4,
        scratch_shapes=[pltpu.VMEM(out.shape, out.dtype) for out in outs] + [dma((2, 4))],
        name="place_outputs",
    )(*outs)
    return (outs[0], outs[1], outs[2], outs[3].T)


def solution(mesh):
    placed = (
        P(("dp", "tensor"), None),
        P("tensor", "dp"),
        P("dp", "tensor"),
        P("dp", "tensor"),
        P("dp", "tensor"),
        P("dp"),
    )
    return jax.shard_map(
        on_device,
        mesh=mesh,
        in_specs=placed,
        out_specs=(P("dp", "tensor"), P("dp", "tensor"), P("dp", "tensor"), P("tensor", "dp")),
        check_vma=False,
    )
```

```python
import jax
import jax.numpy as jnp
from jax import lax
from jax.sharding import PartitionSpec as P
import jax.experimental.pallas as pl
import jax.experimental.pallas.tpu as pltpu

HDIM = 128
BUCKET = 512
ROWS = 1024
SUB = 128
WIDTH = 6144
COLS = 384
SHARD = 192
STEPS = 16
AHEAD = 5
MESH = pl.DeviceIdType.MESH
BF = jnp.bfloat16
F32 = jnp.float32
masked_value = -1e30
score_scale = HDIM ** (-0.5)


def dot(a, b, da, db):
    return lax.dot_general(a, b, (((da,), (db,)), ((), ())), preferred_element_type=F32)


def kernel(
    grad_hbm, q_hbm, k_hbm, v_hbm, weight_ref, ids_ref,
    dq_hbm, dk_hbm, dv_hbm, wg_ref,
    grad, weight, attn_t, prob_t, head_grad, stage, parts, pair_out, pair_in, early_sum,
    q_ref, k_ref, v_ref, dq_ref, dk_ref, dv_ref, local_sem, in_sem, out_sem, hop_send, hop_recv, sib_send, sib_recv,
    w_send, w_recv, part_send, part_recv, pair_send, pair_recv,
):
    dp = lax.axis_index("dp")
    tensor = lax.axis_index("tensor")
    zl, x, y = dp // 16, (dp // 4) % 4, dp % 4
    zh, core = tensor // 2, tensor % 2
    here = x * 4 + y
    u, v = jnp.where(core == 0, x, y), jnp.where(core == 0, y, x)
    up, down, far = (zh + 1) % 4, (zh + 3) % 4, (zh + 2) % 4
    ahead, back = jnp.where(core == 0, up, down), jnp.where(core == 0, down, up)
    next_id = (dp, ahead * 2 + core)
    up_id, down_id = (dp, up * 2 + core), (dp, down * 2 + core)
    sib_id = (dp, zh * 2 + 1 - core)
    pair_id = ((1 - zl) * 16 + here, tensor)

    def plane_id(px, py):
        return (zl * 16 + px * 4 + py, tensor)

    def remote(src, dst, send, recv, device):
        return pltpu.make_async_remote_copy(
            src_ref=src, dst_ref=dst, send_sem=send, recv_sem=recv,
            device_id=device, device_id_type=MESH,
        )

    def place(s):
        group = s // 8
        zc = jnp.where(group == 0, 1 - zl, zl)
        xc = (x + 3 - (s % 8) // 2) % 4
        half = (s + 1 + y // 2) % 2
        return group, zc, xc, half

    def chunk(s):
        _, zc, xc, half = place(s)
        return (zc * 4 + xc) * 2 + half

    def block(z, s, first=0, rows=SUB):
        start = pl.multiple_of((z * 2 + core) * SUB + first, rows)
        return grad.at[chunk(s), pl.ds(start, rows), :]

    def hop_copy(s, n):
        part = block((zh, back, far)[n], s)
        return remote(part, part, hop_send.at[n, s], hop_recv.at[n, s], next_id)

    def hop_arrival(s, n):
        part = block((back, far, ahead)[n], s)
        return remote(part, part, hop_send.at[n, s], hop_recv.at[n, s], next_id)

    def sib_copy(s, n):
        part = block((zh, back, far, ahead)[n], s)
        return remote(part, part, sib_send.at[n, s], sib_recv.at[n, s], sib_id)

    def sib_arrival(s, n):
        z = (zh, back, far, ahead)[n]
        start = pl.multiple_of((z * 2 + 1 - core) * SUB, SUB)
        part = grad.at[chunk(s), pl.ds(start, SUB), :]
        return remote(part, part, sib_send.at[n, s], sib_recv.at[n, s], sib_id)

    def w_slot(slot):
        return weight.at[pl.ds(pl.multiple_of(slot * SHARD, SHARD), SHARD), :]

    def spot(u_at, v_at):
        return jnp.where(core == 0, u_at * 4 + v_at, v_at * 4 + u_at)

    def w_copy(group, m):
        zc = jnp.where(group == 0, 1 - zl, zl)
        first = m // 4 == 0
        slot = w_slot(zc * 16 + spot(u, jnp.where(first, v, (v + m) % 4)))
        to = spot((u + m // 4) % 4, jnp.where(first, (v + m) % 4, v))
        return remote(
            slot, slot, w_send.at[group, m],
            w_recv.at[zc * 16 + spot(u, jnp.where(first, v, (v + m) % 4))], (zl * 16 + to, tensor),
        )

    def w_first(group):
        for m in range(1, 4):
            w_copy(group, m).start()

    def w_second(group):
        zc = jnp.where(group == 0, 1 - zl, zl)
        for m in range(1, 4):
            w_arrival(zc * 16 + spot(u, (v + m) % 4)).wait_recv()

        @pl.loop(4, 16)
        def _(m):
            w_copy(group, m).start()

    def pair_w():
        slot = dp
        return remote(w_slot(slot), w_slot(slot), w_send.at[1, 0], w_recv.at[slot], pair_id)

    def w_arrival(slot):
        return remote(w_slot(slot), w_slot(slot), w_send.at[0, 0], w_recv.at[slot], pair_id)

    def part_copy(s, n):
        group, zc, xc, half = place(s)
        return remote(
            stage.at[s, pl.ds(n * SHARD, SHARD), :], parts.at[group, here],
            part_send.at[s, n], part_recv.at[group, here], plane_id(xc, half * 2 + n),
        )

    def part_arrival(group, source):
        return remote(
            parts.at[group, source], parts.at[group, source],
            part_send.at[0, 0], part_recv.at[group, source], pair_id,
        )

    def pair_copy():
        return remote(pair_out, pair_in, pair_send, pair_recv, pair_id)

    def load(s):
        return pltpu.make_async_copy(
            grad_hbm.at[:, pl.ds(pl.multiple_of(chunk(s) * COLS, COLS), COLS)],
            block(zh, s), local_sem.at[s],
        )

    @pl.loop(0, STEPS)
    def _(s):
        load(s).start()

    heads_in = [
        pltpu.make_async_copy(src, dst, in_sem.at[n])
        for n, (src, dst) in enumerate(((q_hbm, q_ref), (k_hbm, k_ref), (v_hbm, v_ref)))
    ]
    heads_out = [
        pltpu.make_async_copy(src, dst, out_sem.at[n])
        for n, (src, dst) in enumerate(((dq_ref, dq_hbm), (dk_ref, dk_hbm), (dv_ref, dv_hbm)))
    ]
    barrier = pltpu.get_barrier_semaphore()
    for device in (up_id, down_id, sib_id, pair_id):
        pl.semaphore_signal(barrier, inc=1, device_id=device, device_id_type=MESH)
    for m in range(16):
        if m != 12:
            pl.semaphore_signal(
                barrier, inc=1, device_id=plane_id((x + 1 + m // 4) % 4, (y + m) % 4),
                device_id_type=MESH,
            )
    for copy in heads_in:
        copy.start()
    weight[pl.ds(pl.multiple_of(dp * SHARD, SHARD), SHARD), :] = weight_ref[...]
    @pl.loop(0, STEPS)
    def _(s):
        load(s).wait()

    pl.semaphore_wait(barrier, 19)

    hop_copy(0, 0).start()
    pair_w().start()
    w_first(1)

    @pl.loop(1, AHEAD)
    def _(s):
        hop_copy(s, 0).start()

    def head_slices(i):
        bucket, head = i // 3, i % 3
        rows = pl.ds(pl.multiple_of(bucket * BUCKET, BUCKET), BUCKET)
        cols = pl.ds(pl.multiple_of(head * HDIM, HDIM), HDIM)
        return bucket, rows, cols

    for copy in heads_in:
        copy.wait()

    @pl.loop(0, 6)
    def _(i):
        bucket, rows, cols = head_slices(i)
        ids = ids_ref[bucket]
        position = lax.broadcasted_iota(jnp.int32, (1, BUCKET), 1)
        label = jnp.where(ids < 0, -1 - position, ids).astype(F32)
        column = jnp.broadcast_to(label, (HDIM, BUCKET)).T
        column = jnp.concatenate([column] * (BUCKET // HDIM), axis=1)
        scores = dot(k_ref[rows, cols], q_ref[rows, cols], 1, 1) * score_scale
        scores = jnp.where(column == label, scores, masked_value)
        weights = jnp.exp(scores - jnp.max(scores, axis=0, keepdims=True))
        prob = weights / jnp.sum(weights, axis=0, keepdims=True)
        prob_t[i] = prob
        attn_t[cols, rows] = dot(v_ref[rows, cols], prob.astype(BF), 0, 0).astype(BF)

    head_grad[...] = jnp.zeros_like(head_grad)

    def weight_part(s):
        at = chunk(s)
        group, zc, xc, half = place(s)
        for h in range(3):
            part = dot(attn_t[h * HDIM:(h + 1) * HDIM, :], grad[at], 1, 0)
            stage[s, :, h * HDIM:(h + 1) * HDIM] = part.T.astype(BF)
        for n in range(2):
            mine = (xc == x) & (half * 2 + n == y)

            @pl.when(mine)
            def _():
                parts[group, here] = stage[s, n * SHARD:(n + 1) * SHARD, :]

            @pl.when(jnp.logical_not(mine))
            def _():
                part_copy(s, n).start()

    def head_part(s):
        at = chunk(s)
        group, zc, xc, half = place(s)
        for n in range(2):
            yc = half * 2 + n

            @pl.when(jnp.where(core == 0, xc, yc) != u)
            def _():
                w_arrival(zc * 16 + xc * 4 + yc).wait_recv()

        w_part = weight[pl.ds(pl.multiple_of(at * COLS, COLS), COLS), :]
        for t in range(4):
            rows = pl.ds(t * 256, 256)
            head_grad[rows, :] += dot(grad[at, rows, :], w_part, 1, 0)

    def source_at(i):
        return ((x + 1 + i // 4) % 4) * 4 + i % 4

    def collect(group, first, last):
        @pl.loop(first, last)
        def _(i):
            @pl.when(source_at(i) != here)
            def _():
                part_arrival(group, source_at(i)).wait_recv()

    def part_sum(group, rows, first, last):
        def add(i, total):
            return total + parts[group, source_at(i), rows, :].astype(F32)

        return lax.fori_loop(first, last, add, jnp.zeros((48, COLS), F32))

    def sent(s):
        for n in range(3):
            hop_copy(s, n).wait_send()
        for n in range(4):
            sib_copy(s, n).wait_send()
        group, zc, xc, half = place(s)
        for n in range(2):
            @pl.when((xc != x) | (half * 2 + n != y))
            def _():
                part_copy(s, n).wait_send()

    @pl.loop(0, STEPS + 3)
    def _(s):
        @pl.when(s < STEPS)
        def _():
            hop_arrival(s, 0).wait_recv()
            hop_copy(s, 1).start()
            sib_copy(s, 0).start()
            sib_copy(s, 1).start()

        @pl.when((s >= 1) & (s <= STEPS))
        def _():
            hop_arrival(s - 1, 1).wait_recv()
            hop_copy(s - 1, 2).start()
            sib_copy(s - 1, 2).start()

        @pl.when(s == 1)
        def _():
            w_arrival((1 - zl) * 16 + here).wait_recv()
            w_first(0)

        @pl.when(s == 3)
        def _():
            w_second(0)

        @pl.when(s == 5)
        def _():
            w_second(1)

        @pl.when(s + AHEAD < STEPS)
        def _():
            hop_copy(s + AHEAD, 0).start()

        @pl.when((s >= 2) & (s < STEPS + 2))
        def _():
            hop_arrival(s - 2, 2).wait_recv()
            sib_copy(s - 2, 3).start()

        @pl.when(s >= 3)
        def _():
            t = s - 3
            for n in range(4):
                sib_arrival(t, n).wait_recv()
            weight_part(t)

        @pl.when(s >= 8)
        def _():
            catch_up = s <= 12

            @pl.loop(jnp.where(catch_up, 2 * s - 16, s - 3), jnp.where(catch_up, 2 * s - 14, s - 2))
            def _(r):
                head_part(r)

        @pl.when(s == 13)
        def _():
            pair_w().wait_send()

            @pl.loop(1, 16)
            def _(m):
                w_copy(0, m).wait_send()
                w_copy(1, m).wait_send()

        @pl.when(s == 13)
        def _():
            collect(0, 0, 16)

            @pl.loop(0, 4)
            def _(r):
                rows = pl.ds(pl.multiple_of(r * 48, 48), 48)
                pair_out[rows, :] = part_sum(0, rows, 0, 16).astype(BF)

            pair_copy().start()

        @pl.when(s == STEPS + 1)
        def _():
            collect(1, 0, 12)

            @pl.loop(0, 4)
            def _(r):
                rows = pl.ds(pl.multiple_of(r * 48, 48), 48)
                early_sum[rows, :] = part_sum(1, rows, 0, 12)

    @pl.loop(0, 6, unroll=2)
    def _(i):
        bucket, rows, cols = head_slices(i)
        grad_h = head_grad[rows, cols].astype(BF)
        prob = prob_t[i]
        prob_grad = dot(v_ref[rows, cols], grad_h, 1, 1)
        delta = jnp.sum(
            grad_h.astype(F32).T * attn_t[cols, rows].astype(F32), axis=0, keepdims=True
        )
        score_grad = (prob * (prob_grad - delta)).astype(BF)
        dv_ref[rows, cols] = dot(prob.astype(BF), grad_h, 1, 0).astype(BF)
        dk_ref[rows, cols] = (dot(score_grad, q_ref[rows, cols], 1, 0) * score_scale).astype(BF)
        dq = dot(k_ref[rows, cols], score_grad, 0, 0) * score_scale
        dq_ref[rows, cols] = dq.T.astype(BF)

    for copy in heads_out:
        copy.start()
    collect(1, 12, 16)
    pair_copy().wait_recv()

    @pl.loop(0, 4)
    def _(r):
        rows = pl.ds(pl.multiple_of(r * 48, 48), 48)
        late = part_sum(1, rows, 12, 16) + pair_in[rows, :].astype(F32)
        wg_ref[rows, :] = early_sum[rows, :] + late

    for copy in heads_out:
        copy.wait()
    pair_copy().wait_send()

    @pl.loop(0, STEPS)
    def _(s):
        sent(s)


def place_outputs(*refs):
    ins, outs, held, sems = refs[:4], refs[4:8], refs[8:12], refs[12]
    loads = [pltpu.make_async_copy(ins[n], held[n], sems.at[0, n]) for n in range(4)]
    stores = [pltpu.make_async_copy(held[n], outs[n], sems.at[1, n]) for n in range(4)]
    for copy in loads:
        copy.start()
    for n in range(4):
        loads[n].wait()
        stores[n].start()
    for copy in stores:
        copy.wait()


def on_device(grad_out, out_weight, queries, keys_in, values, image_ids):
    vmem = pl.BlockSpec(memory_space=pltpu.VMEM)
    hbm = pl.BlockSpec(memory_space=pl.ANY)
    dma = pltpu.SemaphoreType.DMA
    outs = pl.pallas_call(
        kernel,
        out_shape=(
            jax.ShapeDtypeStruct((ROWS, COLS), BF),
            jax.ShapeDtypeStruct((ROWS, COLS), BF),
            jax.ShapeDtypeStruct((ROWS, COLS), BF),
            jax.ShapeDtypeStruct((SHARD, COLS), F32),
        ),
        in_specs=[hbm] * 4 + [vmem] * 2,
        out_specs=(hbm,) * 3 + (vmem,),
        scratch_shapes=[
            pltpu.VMEM((STEPS, ROWS, COLS), BF),
            pltpu.VMEM((WIDTH, COLS), BF),
            pltpu.VMEM((COLS, ROWS), BF),
            pltpu.VMEM((6, BUCKET, BUCKET), F32),
            pltpu.VMEM((ROWS, COLS), F32),
            pltpu.VMEM((STEPS, COLS, COLS), BF),
            pltpu.VMEM((2, 16, SHARD, COLS), BF),
            pltpu.VMEM((SHARD, COLS), BF),
            pltpu.VMEM((SHARD, COLS), BF),
            pltpu.VMEM((SHARD, COLS), F32),
        ] + [pltpu.VMEM((ROWS, COLS), BF)] * 6 + [
            dma((STEPS,)), dma((3,)), dma((3,)),
            dma((3, STEPS)), dma((3, STEPS)),
            dma((4, STEPS)), dma((4, STEPS)),
            dma((2, 16)), dma((32,)),
            dma((STEPS, 2)), dma((2, 16)),
            dma, dma,
        ],
        compiler_params=pltpu.CompilerParams(
            collective_id=0, has_side_effects=True, vmem_limit_bytes=60 * 2**20
        ),
        cost_estimate=pl.CostEstimate(
            flops=13 * 10**9, bytes_accessed=30 * 10**6, transcendentals=1572864
        ),
        name="attention_backward",
    )(
        grad_out, queries, keys_in, values, out_weight.T,
        image_ids.reshape(2, 1, BUCKET),
    )
    outs = pl.pallas_call(
        place_outputs,
        out_shape=tuple(jax.ShapeDtypeStruct(out.shape, out.dtype) for out in outs),
        in_specs=[hbm] * 4,
        out_specs=(hbm,) * 4,
        scratch_shapes=[pltpu.VMEM(out.shape, out.dtype) for out in outs] + [dma((2, 4))],
        name="place_outputs",
    )(*outs)
    return (outs[0], outs[1], outs[2], outs[3].T)


def solution(mesh):
    placed = (
        P(("dp", "tensor"), None),
        P("tensor", "dp"),
        P("dp", "tensor"),
        P("dp", "tensor"),
        P("dp", "tensor"),
        P("dp"),
    )
    return jax.shard_map(
        on_device,
        mesh=mesh,
        in_specs=placed,
        out_specs=(P("dp", "tensor"), P("dp", "tensor"), P("dp", "tensor"), P("tensor", "dp")),
        check_vma=False,
    )
```

```python
import jax
import jax.numpy as jnp
from jax import lax
from jax.sharding import PartitionSpec as P
import jax.experimental.pallas as pl
import jax.experimental.pallas.tpu as pltpu

HDIM = 128
BUCKET = 512
ROWS = 1024
SUB = 128
WIDTH = 6144
COLS = 384
SHARD = 192
STEPS = 16
AHEAD = 5
MESH = pl.DeviceIdType.MESH
BF = jnp.bfloat16
F32 = jnp.float32
masked_value = -1e30
score_scale = HDIM ** (-0.5)


def dot(a, b, da, db):
    return lax.dot_general(a, b, (((da,), (db,)), ((), ())), preferred_element_type=F32)


def kernel(
    grad_hbm, q_hbm, k_hbm, v_hbm, weight_ref, ids_ref,
    dq_hbm, dk_hbm, dv_hbm, wg_ref,
    grad, weight, attn_t, prob_t, head_grad, stage, parts, pair_out, pair_in, early_sum,
    q_ref, k_ref, v_ref, dq_ref, dk_ref, dv_ref, local_sem, in_sem, out_sem, hop_send, hop_recv, sib_send, sib_recv,
    w_send, w_recv, part_send, part_recv, pair_send, pair_recv,
):
    dp = lax.axis_index("dp")
    tensor = lax.axis_index("tensor")
    zl, x, y = dp // 16, (dp // 4) % 4, dp % 4
    zh, core = tensor // 2, tensor % 2
    here = x * 4 + y
    u, v = jnp.where(core == 0, x, y), jnp.where(core == 0, y, x)
    up, down, far = (zh + 1) % 4, (zh + 3) % 4, (zh + 2) % 4
    ahead, back = jnp.where(core == 0, up, down), jnp.where(core == 0, down, up)
    next_id = (dp, ahead * 2 + core)
    up_id, down_id = (dp, up * 2 + core), (dp, down * 2 + core)
    sib_id = (dp, zh * 2 + 1 - core)
    pair_id = ((1 - zl) * 16 + here, tensor)

    def plane_id(px, py):
        return (zl * 16 + px * 4 + py, tensor)

    def remote(src, dst, send, recv, device):
        return pltpu.make_async_remote_copy(
            src_ref=src, dst_ref=dst, send_sem=send, recv_sem=recv,
            device_id=device, device_id_type=MESH,
        )

    def place(s):
        group = s // 8
        zc = jnp.where(group == 0, 1 - zl, zl)
        xc = (x + 3 - (s % 8) // 2) % 4
        half = (s + 1 + y // 2) % 2
        return group, zc, xc, half

    def chunk(s):
        _, zc, xc, half = place(s)
        return (zc * 4 + xc) * 2 + half

    def block(z, s, first=0, rows=SUB):
        start = pl.multiple_of((z * 2 + core) * SUB + first, rows)
        return grad.at[chunk(s), pl.ds(start, rows), :]

    def hop_copy(s, n):
        part = block((zh, back, far)[n], s)
        return remote(part, part, hop_send.at[n, s], hop_recv.at[n, s], next_id)

    def hop_arrival(s, n):
        part = block((back, far, ahead)[n], s)
        return remote(part, part, hop_send.at[n, s], hop_recv.at[n, s], next_id)

    def sib_copy(s, n):
        part = block((zh, back, far, ahead)[n], s)
        return remote(part, part, sib_send.at[n, s], sib_recv.at[n, s], sib_id)

    def sib_arrival(s, n):
        z = (zh, back, far, ahead)[n]
        start = pl.multiple_of((z * 2 + 1 - core) * SUB, SUB)
        part = grad.at[chunk(s), pl.ds(start, SUB), :]
        return remote(part, part, sib_send.at[n, s], sib_recv.at[n, s], sib_id)

    def w_slot(slot):
        return weight.at[pl.ds(pl.multiple_of(slot * SHARD, SHARD), SHARD), :]

    def spot(u_at, v_at):
        return jnp.where(core == 0, u_at * 4 + v_at, v_at * 4 + u_at)

    def w_copy(group, m):
        zc = jnp.where(group == 0, 1 - zl, zl)
        first = m // 4 == 0
        slot = w_slot(zc * 16 + spot(u, jnp.where(first, v, (v + m) % 4)))
        to = spot((u + m // 4) % 4, jnp.where(first, (v + m) % 4, v))
        return remote(
            slot, slot, w_send.at[group, m],
            w_recv.at[zc * 16 + spot(u, jnp.where(first, v, (v + m) % 4))], (zl * 16 + to, tensor),
        )

    def w_first(group):
        for m in range(1, 4):
            w_copy(group, m).start()

    def w_second(group):
        zc = jnp.where(group == 0, 1 - zl, zl)
        for m in range(1, 4):
            w_arrival(zc * 16 + spot(u, (v + m) % 4)).wait_recv()

        @pl.loop(4, 16)
        def _(m):
            w_copy(group, m).start()

    def pair_w():
        slot = dp
        return remote(w_slot(slot), w_slot(slot), w_send.at[1, 0], w_recv.at[slot], pair_id)

    def w_arrival(slot):
        return remote(w_slot(slot), w_slot(slot), w_send.at[0, 0], w_recv.at[slot], pair_id)

    def part_copy(s, n):
        group, zc, xc, half = place(s)
        return remote(
            stage.at[s, pl.ds(n * SHARD, SHARD), :], parts.at[group, here],
            part_send.at[s, n], part_recv.at[group, here], plane_id(xc, half * 2 + n),
        )

    def part_arrival(group, source):
        return remote(
            parts.at[group, source], parts.at[group, source],
            part_send.at[0, 0], part_recv.at[group, source], pair_id,
        )

    def pair_copy():
        return remote(pair_out, pair_in, pair_send, pair_recv, pair_id)

    def load(s):
        return pltpu.make_async_copy(
            grad_hbm.at[:, pl.ds(pl.multiple_of(chunk(s) * COLS, COLS), COLS)],
            block(zh, s), local_sem.at[s],
        )

    @pl.loop(0, STEPS)
    def _(s):
        load(s).start()

    heads_in = [
        pltpu.make_async_copy(src, dst, in_sem.at[n])
        for n, (src, dst) in enumerate(((q_hbm, q_ref), (k_hbm, k_ref), (v_hbm, v_ref)))
    ]
    heads_out = [
        pltpu.make_async_copy(src, dst, out_sem.at[n])
        for n, (src, dst) in enumerate(((dq_ref, dq_hbm), (dk_ref, dk_hbm), (dv_ref, dv_hbm)))
    ]
    barrier = pltpu.get_barrier_semaphore()
    for device in (up_id, down_id, sib_id, pair_id):
        pl.semaphore_signal(barrier, inc=1, device_id=device, device_id_type=MESH)
    for m in range(16):
        if m != 12:
            pl.semaphore_signal(
                barrier, inc=1, device_id=plane_id((x + 1 + m // 4) % 4, (y + m) % 4),
                device_id_type=MESH,
            )
    for copy in heads_in:
        copy.start()
    weight[pl.ds(pl.multiple_of(dp * SHARD, SHARD), SHARD), :] = weight_ref[...]
    @pl.loop(0, STEPS)
    def _(s):
        load(s).wait()

    pl.semaphore_wait(barrier, 19)

    hop_copy(0, 0).start()
    pair_w().start()
    w_first(1)

    @pl.loop(1, AHEAD)
    def _(s):
        hop_copy(s, 0).start()

    def head_slices(i):
        bucket, head = i // 3, i % 3
        rows = pl.ds(pl.multiple_of(bucket * BUCKET, BUCKET), BUCKET)
        cols = pl.ds(pl.multiple_of(head * HDIM, HDIM), HDIM)
        return bucket, rows, cols

    for copy in heads_in:
        copy.wait()

    @pl.loop(0, 6)
    def _(i):
        bucket, rows, cols = head_slices(i)
        ids = ids_ref[bucket]
        position = lax.broadcasted_iota(jnp.int32, (1, BUCKET), 1)
        label = jnp.where(ids < 0, -1 - position, ids).astype(F32)
        column = jnp.broadcast_to(label, (HDIM, BUCKET)).T
        column = jnp.concatenate([column] * (BUCKET // HDIM), axis=1)
        scores = dot(k_ref[rows, cols], q_ref[rows, cols], 1, 1) * score_scale
        scores = jnp.where(column == label, scores, masked_value)
        weights = jnp.exp(scores - jnp.max(scores, axis=0, keepdims=True))
        prob = weights / jnp.sum(weights, axis=0, keepdims=True)
        prob_t[i] = prob
        attn_t[cols, rows] = dot(v_ref[rows, cols], prob.astype(BF), 0, 0).astype(BF)

    head_grad[...] = jnp.zeros_like(head_grad)

    def weight_part(s):
        at = chunk(s)
        group, zc, xc, half = place(s)
        for h in range(3):
            part = dot(attn_t[h * HDIM:(h + 1) * HDIM, :], grad[at], 1, 0)
            stage[s, :, h * HDIM:(h + 1) * HDIM] = part.T.astype(BF)
        for n in range(2):
            mine = (xc == x) & (half * 2 + n == y)

            @pl.when(mine)
            def _():
                parts[group, here] = stage[s, n * SHARD:(n + 1) * SHARD, :]

            @pl.when(jnp.logical_not(mine))
            def _():
                part_copy(s, n).start()

    def head_part(s):
        at = chunk(s)
        group, zc, xc, half = place(s)
        for n in range(2):
            yc = half * 2 + n

            @pl.when(jnp.where(core == 0, xc, yc) != u)
            def _():
                w_arrival(zc * 16 + xc * 4 + yc).wait_recv()

        w_part = weight[pl.ds(pl.multiple_of(at * COLS, COLS), COLS), :]
        for t in range(4):
            rows = pl.ds(t * 256, 256)
            head_grad[rows, :] += dot(grad[at, rows, :], w_part, 1, 0)

    def source_at(i):
        return ((x + 1 + i // 4) % 4) * 4 + i % 4

    def collect(group, first, last):
        @pl.loop(first, last)
        def _(i):
            @pl.when(source_at(i) != here)
            def _():
                part_arrival(group, source_at(i)).wait_recv()

    def part_sum(group, rows, first, last):
        def add(i, total):
            return total + parts[group, source_at(i), rows, :].astype(F32)

        return lax.fori_loop(first, last, add, jnp.zeros((48, COLS), F32))

    def sent(s):
        for n in range(3):
            hop_copy(s, n).wait_send()
        for n in range(4):
            sib_copy(s, n).wait_send()
        group, zc, xc, half = place(s)
        for n in range(2):
            @pl.when((xc != x) | (half * 2 + n != y))
            def _():
                part_copy(s, n).wait_send()

    @pl.loop(0, STEPS + 3)
    def _(s):
        @pl.when(s < STEPS)
        def _():
            hop_arrival(s, 0).wait_recv()
            hop_copy(s, 1).start()
            sib_copy(s, 0).start()
            sib_copy(s, 1).start()

        @pl.when((s >= 1) & (s <= STEPS))
        def _():
            hop_arrival(s - 1, 1).wait_recv()
            hop_copy(s - 1, 2).start()
            sib_copy(s - 1, 2).start()

        @pl.when(s == 1)
        def _():
            w_arrival((1 - zl) * 16 + here).wait_recv()
            w_first(0)

        @pl.when(s == 3)
        def _():
            w_second(0)

        @pl.when(s == 5)
        def _():
            w_second(1)

        @pl.when(s + AHEAD < STEPS)
        def _():
            hop_copy(s + AHEAD, 0).start()

        @pl.when((s >= 2) & (s < STEPS + 2))
        def _():
            hop_arrival(s - 2, 2).wait_recv()
            sib_copy(s - 2, 3).start()

        @pl.when(s >= 3)
        def _():
            t = s - 3
            for n in range(4):
                sib_arrival(t, n).wait_recv()
            weight_part(t)

        @pl.when(s >= 8)
        def _():
            catch_up = s <= 12

            @pl.loop(jnp.where(catch_up, 2 * s - 16, s - 3), jnp.where(catch_up, 2 * s - 14, s - 2))
            def _(r):
                head_part(r)

        @pl.when(s == 13)
        def _():
            pair_w().wait_send()

            @pl.loop(1, 16)
            def _(m):
                w_copy(0, m).wait_send()
                w_copy(1, m).wait_send()

        @pl.when(s == 13)
        def _():
            collect(0, 0, 16)

            @pl.loop(0, 4)
            def _(r):
                rows = pl.ds(pl.multiple_of(r * 48, 48), 48)
                pair_out[rows, :] = part_sum(0, rows, 0, 16).astype(BF)

            pair_copy().start()

        @pl.when(s == STEPS + 2)
        def _():
            collect(1, 0, 12)

            @pl.loop(0, 4)
            def _(r):
                rows = pl.ds(pl.multiple_of(r * 48, 48), 48)
                early_sum[rows, :] = part_sum(1, rows, 0, 12)

    @pl.loop(0, 6, unroll=2)
    def _(i):
        bucket, rows, cols = head_slices(i)
        grad_h = head_grad[rows, cols].astype(BF)
        prob = prob_t[i]
        prob_grad = dot(v_ref[rows, cols], grad_h, 1, 1)
        delta = jnp.sum(
            grad_h.astype(F32).T * attn_t[cols, rows].astype(F32), axis=0, keepdims=True
        )
        score_grad = (prob * (prob_grad - delta)).astype(BF)
        dv_ref[rows, cols] = dot(prob.astype(BF), grad_h, 1, 0).astype(BF)
        dk_ref[rows, cols] = (dot(score_grad, q_ref[rows, cols], 1, 0) * score_scale).astype(BF)
        dq = dot(k_ref[rows, cols], score_grad, 0, 0) * score_scale
        dq_ref[rows, cols] = dq.T.astype(BF)

    for copy in heads_out:
        copy.start()
    collect(1, 12, 16)
    pair_copy().wait_recv()

    @pl.loop(0, 4)
    def _(r):
        rows = pl.ds(pl.multiple_of(r * 48, 48), 48)
        late = part_sum(1, rows, 12, 16) + pair_in[rows, :].astype(F32)
        wg_ref[rows, :] = early_sum[rows, :] + late

    for copy in heads_out:
        copy.wait()
    pair_copy().wait_send()

    @pl.loop(0, STEPS)
    def _(s):
        sent(s)


def place_outputs(*refs):
    ins, outs, held, sems = refs[:4], refs[4:8], refs[8:12], refs[12]
    loads = [pltpu.make_async_copy(ins[n], held[n], sems.at[0, n]) for n in range(4)]
    stores = [pltpu.make_async_copy(held[n], outs[n], sems.at[1, n]) for n in range(4)]
    for copy in loads:
        copy.start()
    for n in range(4):
        loads[n].wait()
        stores[n].start()
    for copy in stores:
        copy.wait()


def on_device(grad_out, out_weight, queries, keys_in, values, image_ids):
    vmem = pl.BlockSpec(memory_space=pltpu.VMEM)
    hbm = pl.BlockSpec(memory_space=pl.ANY)
    dma = pltpu.SemaphoreType.DMA
    outs = pl.pallas_call(
        kernel,
        out_shape=(
            jax.ShapeDtypeStruct((ROWS, COLS), BF),
            jax.ShapeDtypeStruct((ROWS, COLS), BF),
            jax.ShapeDtypeStruct((ROWS, COLS), BF),
            jax.ShapeDtypeStruct((SHARD, COLS), F32),
        ),
        in_specs=[hbm] * 4 + [vmem] * 2,
        out_specs=(hbm,) * 3 + (vmem,),
        scratch_shapes=[
            pltpu.VMEM((STEPS, ROWS, COLS), BF),
            pltpu.VMEM((WIDTH, COLS), BF),
            pltpu.VMEM((COLS, ROWS), BF),
            pltpu.VMEM((6, BUCKET, BUCKET), F32),
            pltpu.VMEM((ROWS, COLS), F32),
            pltpu.VMEM((STEPS, COLS, COLS), BF),
            pltpu.VMEM((2, 16, SHARD, COLS), BF),
            pltpu.VMEM((SHARD, COLS), BF),
            pltpu.VMEM((SHARD, COLS), BF),
            pltpu.VMEM((SHARD, COLS), F32),
        ] + [pltpu.VMEM((ROWS, COLS), BF)] * 6 + [
            dma((STEPS,)), dma((3,)), dma((3,)),
            dma((3, STEPS)), dma((3, STEPS)),
            dma((4, STEPS)), dma((4, STEPS)),
            dma((2, 16)), dma((32,)),
            dma((STEPS, 2)), dma((2, 16)),
            dma, dma,
        ],
        compiler_params=pltpu.CompilerParams(
            collective_id=0, has_side_effects=True, vmem_limit_bytes=60 * 2**20
        ),
        cost_estimate=pl.CostEstimate(
            flops=13 * 10**9, bytes_accessed=30 * 10**6, transcendentals=1572864
        ),
        name="attention_backward",
    )(
        grad_out, queries, keys_in, values, out_weight.T,
        image_ids.reshape(2, 1, BUCKET),
    )
    outs = pl.pallas_call(
        place_outputs,
        out_shape=tuple(jax.ShapeDtypeStruct(out.shape, out.dtype) for out in outs),
        in_specs=[hbm] * 4,
        out_specs=(hbm,) * 4,
        scratch_shapes=[pltpu.VMEM(out.shape, out.dtype) for out in outs] + [dma((2, 4))],
        name="place_outputs",
    )(*outs)
    return (outs[0], outs[1], outs[2], outs[3].T)


def solution(mesh):
    placed = (
        P(("dp", "tensor"), None),
        P("tensor", "dp"),
        P("dp", "tensor"),
        P("dp", "tensor"),
        P("dp", "tensor"),
        P("dp"),
    )
    return jax.shard_map(
        on_device,
        mesh=mesh,
        in_specs=placed,
        out_specs=(P("dp", "tensor"), P("dp", "tensor"), P("dp", "tensor"), P("tensor", "dp")),
        check_vma=False,
    )
```
